32 devices in a mesh: parts: 2 (over x), blk: 8 (over z, y), kvh: 2 (over core).
Axes of the slice: x: 2, y: 2, z: 4, core: 2. Of those that a mesh axis runs over, the one named last changes fastest.
Arguments:
- queries: bfloat16 [512, 5120], P(('parts', 'blk'), 'kvh'), parts along dimension 0, may hold values from -20 to 20
- block_key_cache: bfloat16 [128, 512, 1024], P(('parts', 'blk'), None, 'kvh'), parts along dimension 0, may hold values from -5 to 5
- block_value_cache: bfloat16 [128, 512, 1024], P(('parts', 'blk'), None, 'kvh'), parts along dimension 0, may hold values from -12 to 12
- new_keys: bfloat16 [512, 1024], P(('parts', 'blk'), 'kvh'), parts along dimension 0, may hold values from -9 to 9
- leaf_value_rows: bfloat16 [512, 1024], P(('parts', 'blk'), 'kvh'), parts along dimension 0, may hold values from -12 to 12
- ancestors: int32 [512, 8], P(('parts', 'blk')), parts along dimension 0, may hold values from 0 to 63, as said below
- block_slot: int32 [128], P('parts'), parts along dimension 0, may hold values from 0 to 63, as said below
- last_len: int32 [512], P(('parts', 'blk')), parts along dimension 0, may hold values from 1 to 512
- o_weight: bfloat16 [5120, 5120], P('kvh', 'blk'), may hold values from -0.078125 to 0.078125
Outputs:
- mixed: bfloat16 [512, 5120], P(('parts', 'kvh'), 'blk'), parts along dimension 0
The draws below stay inside these ranges and needn't reach their ends.
There are 2 independent parts, one for each index of `parts`. The reference program is written for one: setup_inputs(seed, part) draws one part's arguments, and reference() takes and returns one part's arrays. A program takes and returns all parts, laid end to end along the dimension named above; an argument that names none is the same for every part. Nothing has to cross between parts.
Inputs may be any that keep to these rules, and one draw needn't show every extreme that they name: `ancestors`: each row names 8 different blocks; the 32 rows of one device name no block more than 8 times. `block_slot`: A permutation: each block has its own row of the caches.
All inputs are finite; a program needn't handle non-finite values.
Results may differ from the reference program's by a relative error of at most 0.0051.
Values may be sent and summed in bfloat16 or wider, within the bound.
A program may use at most 128 MiB of HBM per device.

```python
import math
import jax
import jax.numpy as jnp
from jax import lax

D = 5120
QUERY_HEADS = 40
KEY_VALUE_HEADS = 8
HEAD_SIZE = 128
BLOCK_TOKENS = 512
ANCESTOR_BLOCKS = 8
BLK_DEV = 8
CACHE_BLOCKS = 64
LEAF_TOTAL = 256


def shared_slots(key):
    return jax.random.permutation(jax.random.fold_in(key, 101), CACHE_BLOCKS).astype(jnp.int32)


def base_queries(key):
    return 2.5 * jax.random.truncated_normal(jax.random.fold_in(key, 103), -4.0, 4.0, (LEAF_TOTAL, QUERY_HEADS * HEAD_SIZE), jnp.float32)


def draw_queries(key, part):
    sampled_base = base_queries(key)
    result = sampled_base
    return result.astype(jnp.bfloat16)


def draw_block_key_cache(key, part):
    key = jax.random.fold_in(key, 2)
    array_shape = (CACHE_BLOCKS, BLOCK_TOKENS, KEY_VALUE_HEADS * HEAD_SIZE)
    result = jax.random.truncated_normal(key, -5.0, 5.0, array_shape, jnp.float32)
    return result.astype(jnp.bfloat16)


def draw_new_keys(key, part):
    sampled_base = base_queries(key)
    key = jax.random.fold_in(key, 3)
    grouped_queries = jnp.mean(sampled_base.reshape(LEAF_TOTAL, KEY_VALUE_HEADS, QUERY_HEADS // KEY_VALUE_HEADS, HEAD_SIZE), axis=2)
    random_noise = 0.5 * jax.random.truncated_normal(key, -4.0, 4.0, (LEAF_TOTAL, KEY_VALUE_HEADS, HEAD_SIZE), jnp.float32)
    return (0.7 * grouped_queries + random_noise).reshape(LEAF_TOTAL, KEY_VALUE_HEADS * HEAD_SIZE).astype(jnp.bfloat16)


def draw_block_slot(key, part):
    slot_row_list = shared_slots(key)
    return slot_row_list


def draw_ancestors(key, part):
    slot_of_block = shared_slots(key)
    key = jax.random.fold_in(key, 5)
    catalog = jnp.arange(CACHE_BLOCKS, dtype=jnp.int32)
    block_at_slot = jnp.zeros((CACHE_BLOCKS,), jnp.int32).at[slot_of_block].set(catalog)
    owners = CACHE_BLOCKS // BLK_DEV
    hot_owner = jax.random.randint(jax.random.fold_in(key, 1), (), 0, owners)
    shifted = (catalog - hot_owner * BLK_DEV) % CACHE_BLOCKS
    tier = (CACHE_BLOCKS - 1 - shifted) * 8 // CACHE_BLOCKS
    group_count = 2 * LEAF_TOTAL * ANCESTOR_BLOCKS // CACHE_BLOCKS
    jitter = jax.random.randint(jax.random.fold_in(key, 2), (group_count, CACHE_BLOCKS), 0, 48)
    rating = jnp.where(shifted < BLK_DEV, 100000, tier * 16 + jitter) * CACHE_BLOCKS + catalog
    chosen = lax.top_k(rating.astype(jnp.int32), CACHE_BLOCKS // 2)[1].astype(jnp.int32)
    shuffle_keys = jax.random.split(jax.random.fold_in(key, 3), group_count)
    mixed_order = jax.vmap(jax.random.permutation)(shuffle_keys, chosen)
    return block_at_slot[mixed_order].reshape(LEAF_TOTAL, ANCESTOR_BLOCKS).astype(jnp.int32)


def with_ends(values, own_key, smallest, top_value):
    longest = values.shape.index(max(values.shape))
    spots = []
    for shift in (0, 1):
        where = [jax.random.randint(jax.random.fold_in(own_key, axis), (), 0, length) for axis, length in enumerate(values.shape)]
        where[longest] = (where[longest] + shift) % values.shape[longest]
        spots.append(tuple(where))
    return values.at[spots[0]].set(smallest).at[spots[1]].set(top_value)


def shard_levels(rng, dims, shards, smallest, high):
    level, own = 1.0, jax.random.fold_in(rng, 6)
    for dim, parts in shards:
        draws = jnp.exp(jax.random.uniform(jax.random.fold_in(own, dim), (parts,), jnp.float32, smallest / len(shards), high / len(shards)))
        level = level * jnp.repeat(draws, dims[dim] // parts).reshape([-1 if axis == dim else 1 for axis in range(len(dims))])
    return level


def bell_draw(rng, dims, scale, limit, shards=(), kind=jnp.bfloat16):
    drawn = jax.random.normal(rng, dims, jnp.float32) * scale
    if len(shards) > 0:
        drawn = shard_levels(rng, dims, shards, -0.22, 0.18) * drawn
    return jnp.clip(drawn, min=-limit, max=limit).astype(kind)


def setup_inputs(seed: int = 0, part: int = 0) -> dict:
    key_list = jax.random.split(jax.random.key(seed), 10)
    own_keys = jax.random.split(jax.random.fold_in(key_list[9], part), 10)
    return {
        "queries": draw_queries(jax.random.fold_in(jax.random.fold_in(key_list[9], part), 71), part),
        "block_key_cache": draw_block_key_cache(jax.random.fold_in(jax.random.fold_in(key_list[9], part), 71), part),
        "block_value_cache": bell_draw(own_keys[2], (CACHE_BLOCKS, BLOCK_TOKENS, KEY_VALUE_HEADS * HEAD_SIZE), 2.0, 12.0, ((0, 8), (2, 2))),
        "new_keys": draw_new_keys(jax.random.fold_in(jax.random.fold_in(key_list[9], part), 71), part),
        "leaf_value_rows": bell_draw(own_keys[4], (LEAF_TOTAL, KEY_VALUE_HEADS * HEAD_SIZE), 2.0, 12.0, ((0, 8), (1, 2))),
        "ancestors": draw_ancestors(jax.random.fold_in(jax.random.fold_in(key_list[9], part), 71), part),
        "block_slot": draw_block_slot(jax.random.fold_in(jax.random.fold_in(key_list[9], part), 71), part),
        "last_len": with_ends(jax.random.randint(own_keys[7], (LEAF_TOTAL,), 1, BLOCK_TOKENS + 1), jax.random.fold_in(own_keys[7], 1), 1, BLOCK_TOKENS).astype(jnp.int32),
        "o_weight": bell_draw(key_list[8], (QUERY_HEADS * HEAD_SIZE, D), (QUERY_HEADS * HEAD_SIZE) ** -0.5, 0.078125, ((0, 2), (1, 8))),
    }


def reference(queries, block_key_cache, block_value_cache, new_keys, leaf_value_rows, ancestors, block_slot, last_len, o_weight):
    queries_per_group = QUERY_HEADS // KEY_VALUE_HEADS
    score_scale = 1.0 / math.sqrt(HEAD_SIZE)
    positions = jnp.arange(BLOCK_TOKENS, dtype=jnp.int32)
    levels = jnp.arange(ANCESTOR_BLOCKS, dtype=jnp.int32)

    def one_leaf(leaf_items):
        single_query, leaf_new_key, leaf_new_value, lineage, valid_count = leaf_items
        slot_row_list = block_slot[lineage].astype(jnp.int32)
        gathered_keys = block_key_cache[slot_row_list].astype(jnp.float32).reshape(ANCESTOR_BLOCKS, BLOCK_TOKENS, KEY_VALUE_HEADS, HEAD_SIZE)
        gathered_values = block_value_cache[slot_row_list].astype(jnp.float32).reshape(ANCESTOR_BLOCKS, BLOCK_TOKENS, KEY_VALUE_HEADS, HEAD_SIZE)
        head_row_block = single_query.astype(jnp.float32).reshape(KEY_VALUE_HEADS, queries_per_group, HEAD_SIZE)
        scores = jnp.einsum('geh,nkgh->ngek', head_row_block, gathered_keys) * score_scale
        valid_len = jnp.where(levels == ANCESTOR_BLOCKS - 1, valid_count, BLOCK_TOKENS)
        in_block = positions[None, :] < valid_len[:, None]
        scores = jnp.where(in_block[:, None, None, :], scores, -1e+30)
        block_max = lax.optimization_barrier(jnp.max(scores, axis=-1))
        shares = jnp.exp(scores - block_max[..., None]).astype(jnp.bfloat16)
        shares = lax.optimization_barrier(shares).astype(jnp.float32)
        row_total = lax.optimization_barrier(jnp.sum(shares, axis=-1))
        partial_value = jnp.einsum('ngek,nkgh->ngeh', shares, gathered_values)
        unit = (partial_value / row_total[..., None]).astype(jnp.bfloat16)
        unit = lax.optimization_barrier(unit).astype(jnp.float32)
        own_token_score = jnp.einsum('lnq,lq->ln', head_row_block, leaf_new_key.astype(jnp.float32).reshape(KEY_VALUE_HEADS, HEAD_SIZE)) * score_scale
        overall = jnp.maximum(lax.optimization_barrier(jnp.max(block_max, axis=0)), own_token_score)
        weights = jnp.exp(block_max - overall[None]) * row_total
        own_token_weight = jnp.exp(own_token_score - overall)
        weighted_numerator = lax.optimization_barrier(jnp.sum(weights[..., None] * unit, axis=0))
        weighted_numerator = weighted_numerator + own_token_weight[..., None] * leaf_new_value.astype(jnp.float32).reshape(KEY_VALUE_HEADS, 1, HEAD_SIZE)
        denominator = lax.optimization_barrier(jnp.sum(weights, axis=0)) + own_token_weight
        return (weighted_numerator / denominator[..., None]).reshape(QUERY_HEADS * HEAD_SIZE).astype(jnp.bfloat16)
    attention = lax.map(one_leaf, (queries, new_keys, leaf_value_rows, ancestors, last_len))
    return jnp.dot(attention, o_weight, preferred_element_type=jnp.float32).astype(jnp.bfloat16)
```

```python
import functools
import math

import jax
import jax.numpy as jnp
from jax import lax
from jax.experimental import pallas as pl
from jax.experimental.pallas import tpu as pltpu
from jax.sharding import PartitionSpec as P

QUERY_HEADS = 40
KEY_VALUE_HEADS = 8
HEAD_SIZE = 128
PER_GROUP = QUERY_HEADS // KEY_VALUE_HEADS
ROW_PAIR = 2
SLICES = 1
NEG = -1e30
MESH = pl.DeviceIdType.MESH
F32 = jnp.float32
BF16 = jnp.bfloat16


def dot(a, b):
    return jnp.dot(a, b, preferred_element_type=F32)


def kernel(
    n,
    slices,
    cap,
    q_ref,
    info_ref,
    nk_ref,
    nv_ref,
    key_hbm,
    value_hbm,
    weight_hbm,
    out_ref,
    info_buf,
    q_buf,
    key_buf,
    value_buf,
    weight_buf,
    pick,
    pick_t,
    count,
    unit_buf,
    max_buf,
    total_buf,
    part,
    y_recv,
    merged,
    z_recv,
    att_buf,
    half_send,
    half_recv,
    kv_sem,
    w_sem,
    g_recv,
    g_up,
    g_down,
    g_side,
    y_send_sem,
    y_recv_sem,
    z_send_sem,
    z_recv_sem,
    h_send_sem,
    h_recv_sem,
):
    parts_at = lax.axis_index("parts")
    me = lax.axis_index("blk")
    core = lax.axis_index("kvh")
    nz = n // ROW_PAIR
    z = me // ROW_PAIR
    y = me % ROW_PAIR
    other_y = 1 - y
    leaves = q_ref.shape[0]
    all_leaves = n * leaves
    blocks, block_len, kv_width = key_hbm.shape
    groups = kv_width // HEAD_SIZE
    sg = groups // slices
    heads = sg * PER_GROUP
    width = heads * HEAD_SIZE
    scale = 1.0 / math.sqrt(HEAD_SIZE)
    scale2 = scale * math.log2(math.e)

    def where_is(zz, yy):
        return (parts_at, zz * ROW_PAIR + yy, core)

    kv_copies = []
    for b in range(blocks):
        kv_copies.append(
            (
                pltpu.make_async_copy(key_hbm.at[b], key_buf.at[b], kv_sem.at[0, b]),
                pltpu.make_async_copy(value_hbm.at[b], value_buf.at[b], kv_sem.at[1, b]),
            )
        )

    info_buf[0, me] = info_ref[...]
    for s in range(slices):
        q_buf[s, me] = q_ref[:, s * width : (s + 1) * width]

    barrier = pltpu.get_barrier_semaphore()
    for d in range(1, nz):
        pl.semaphore_signal(
            barrier, inc=1, device_id=where_is((z + d) % nz, y), device_id_type=MESH
        )
    pl.semaphore_signal(barrier, inc=1, device_id=where_is(z, other_y), device_id_type=MESH)
    pl.semaphore_signal(barrier, inc=1, device_id=(parts_at, me, 1 - core), device_id_type=MESH)
    pl.semaphore_wait(barrier, nz + 1)

    def gather_copy(buf, s, row, zz, yy, target, send_sem):
        idx = zz * ROW_PAIR + yy
        return pltpu.make_async_remote_copy(
            src_ref=buf.at[s, idx],
            dst_ref=buf.at[s, idx],
            send_sem=send_sem.at[row, zz],
            recv_sem=g_recv.at[row, idx],
            device_id=target,
            device_id_type=MESH,
        )

    def up_copy(buf, s, row, zz):
        return gather_copy(buf, s, row, zz, y, where_is(jnp.minimum(z + 1, nz - 1), y), g_up)

    def down_copy(buf, s, row, zz):
        return gather_copy(buf, s, row, zz, y, where_is(jnp.maximum(z - 1, 0), y), g_down)

    def side_copy(buf, s, row, zz, yy):
        return gather_copy(buf, s, row, zz, yy, where_is(z, other_y), g_side)

    def gather_start(buf, s, row):
        @pl.when(z < nz - 1)
        def _():
            up_copy(buf, s, row, z).start()

        @pl.when(z > 0)
        def _():
            down_copy(buf, s, row, z).start()

        side_copy(buf, s, row, z, y).start()

    def gather_step(buf, s, row, d):
        @pl.when(z - d >= 0)
        def _():
            zz = z - d
            side_copy(buf, s, row, zz, y).wait_recv()

            @pl.when(z < nz - 1)
            def _():
                up_copy(buf, s, row, zz).start()

            side_copy(buf, s, row, zz, y).start()

        @pl.when(z + d < nz)
        def _():
            zz = z + d
            side_copy(buf, s, row, zz, y).wait_recv()

            @pl.when(z > 0)
            def _():
                down_copy(buf, s, row, zz).start()

            side_copy(buf, s, row, zz, y).start()

    def gather_finish(buf, s, row):
        for zz in range(nz):
            side_copy(buf, s, row, zz, other_y).wait_recv()

    def gather_drain(buf, s, row):
        for zz in range(nz):
            side_copy(buf, s, row, zz, y).wait_send()

            @pl.when((zz <= z) & (z < nz - 1))
            def _():
                up_copy(buf, s, row, zz).wait_send()

            @pl.when((zz >= z) & (z > 0))
            def _():
                down_copy(buf, s, row, zz).wait_send()

    q_row = 1
    a_row = 1 + slices

    gather_start(info_buf, 0, 0)
    for s in range(slices):
        gather_start(q_buf, s, q_row + s)
    for b in range(blocks):
        kv_copies[b][0].start()
        kv_copies[b][1].start()
    weight_copy = pltpu.make_async_copy(weight_hbm, weight_buf, w_sem)
    weight_copy.start()
    for d in range(1, nz):
        gather_step(info_buf, 0, 0, d)
        gather_step(q_buf, 0, q_row, d)
    gather_finish(info_buf, 0, 0)

    info = info_buf[0].astype(F32).reshape(all_leaves, HEAD_SIZE)
    info_t = jnp.transpose(info)
    slots = info_t[0:8]
    last = info_t[8:9] + info_t[9:10]
    level = lax.broadcasted_iota(jnp.int32, (8, all_leaves), 0)
    lengths = jnp.where(level == 7, last, float(block_len))
    base = (me * blocks).astype(F32)
    first = lax.broadcasted_iota(jnp.int32, (8, all_leaves), 0)
    present = jnp.zeros((8, all_leaves), F32)
    valid = jnp.zeros((8, all_leaves), F32)
    for b in range(blocks):
        same = slots == base + float(b)
        here = jnp.sum(jnp.where(same, 1.0, 0.0), axis=0, keepdims=True)
        size = jnp.sum(jnp.where(same, lengths, 0.0), axis=0, keepdims=True)
        present = jnp.where(first == b, here, present)
        valid = jnp.where(first == b, size, valid)
    earlier = (
        lax.broadcasted_iota(jnp.int32, (all_leaves, all_leaves), 0)
        < lax.broadcasted_iota(jnp.int32, (all_leaves, all_leaves), 1)
    )
    rank = dot(present.astype(BF16), jnp.where(earlier, 1.0, 0.0).astype(BF16))
    rank = jnp.where(present > 0.5, rank, -1.0)
    ordinal = lax.broadcasted_iota(jnp.int32, (cap, all_leaves), 0).astype(F32)
    for b in range(blocks):
        chosen = jnp.where(ordinal == rank[b : b + 1], 1.0, 0.0)
        count[b] = jnp.broadcast_to(
            jnp.sum(chosen * valid[b : b + 1], axis=1, keepdims=True), (cap, HEAD_SIZE)
        )
        pick[b] = chosen.astype(BF16)
        pick_t[:, b * cap : (b + 1) * cap] = jnp.transpose(chosen).astype(BF16)

    lane_cap = lax.broadcasted_iota(jnp.int32, (cap, HEAD_SIZE), 1)
    position = lax.broadcasted_iota(jnp.int32, (PER_GROUP * cap, block_len), 1).astype(F32)
    ones = jnp.ones((block_len, HEAD_SIZE), BF16)

    def split_total(value):
        top = value.astype(BF16).astype(F32)
        return top, (value - top).astype(BF16).astype(F32)

    def pack_stats(reference, total):
        top, rest = split_total(total)
        lane = lax.broadcasted_iota(jnp.int32, reference.shape, 1)
        return jnp.where(
            lane < 32,
            reference,
            jnp.where(lane < 64, pltpu.roll(top, 32, 1), pltpu.roll(rest, 64, 1)),
        ).astype(BF16)

    def unpack_stats(stats):
        stats = stats.astype(F32)
        return stats, pltpu.roll(stats, 96, 1) + pltpu.roll(stats, 64, 1)

    def attend(s):
        if s == 0:
            for b in range(blocks):
                kv_copies[b][0].wait()
                kv_copies[b][1].wait()

        def score_block(b, highest):
            choose = pick[b]
            rows = dot(choose, q_buf[s].reshape(all_leaves, width)).astype(BF16)
            limit = count[b][:, 0:1]
            limit = jnp.concatenate([limit] * PER_GROUP, axis=0)
            inside = position < limit
            max_here = jnp.zeros((cap, HEAD_SIZE), F32)
            total_here = jnp.zeros((cap, HEAD_SIZE), F32)
            for g in range(sg):
                at = (s * sg + g) * HEAD_SIZE
                group_rows = jnp.concatenate(
                    [
                        rows[:, (g * PER_GROUP + e) * HEAD_SIZE : (g * PER_GROUP + e + 1) * HEAD_SIZE]
                        for e in range(PER_GROUP)
                    ],
                    axis=0,
                )
                scores = lax.dot_general(
                    group_rows,
                    key_buf[b, :, at : at + HEAD_SIZE],
                    (((1,), (1,)), ((), ())),
                    preferred_element_type=F32,
                )
                scores = jnp.where(inside, scores, NEG)
                top = jnp.max(scores, axis=1, keepdims=True)
                shares = jnp.exp2((scores - top) * scale2).astype(BF16)
                both = dot(
                    shares,
                    jnp.concatenate([value_buf[b, :, at : at + HEAD_SIZE], ones], axis=1),
                )
                sums = both[:, HEAD_SIZE:]
                unit = (both[:, :HEAD_SIZE] / sums).astype(BF16)
                scaled_top = top * scale
                for e in range(PER_GROUP):
                    h = g * PER_GROUP + e
                    unit_buf[b, :, h * HEAD_SIZE : (h + 1) * HEAD_SIZE] = unit[e * cap : (e + 1) * cap]
                    max_here = jnp.where(lane_cap == h, scaled_top[e * cap : (e + 1) * cap], max_here)
                    total_here = jnp.where(lane_cap == h, sums[e * cap : (e + 1) * cap], total_here)
            max_buf[b] = max_here
            total_buf[b] = total_here
            spread = lax.dot_general(
                choose,
                max_here.astype(BF16),
                (((0,), (0,)), ((), ())),
                preferred_element_type=F32,
            )
            have = lax.dot_general(
                choose,
                jnp.ones((cap, HEAD_SIZE), BF16),
                (((0,), (0,)), ((), ())),
                preferred_element_type=F32,
            )
            return jnp.maximum(highest, jnp.where(have > 0.5, spread, NEG))

        highest = lax.fori_loop(
            0, blocks, score_block, jnp.full((all_leaves, HEAD_SIZE), NEG, F32)
        )
        highest = highest.astype(BF16)

        def weigh_block(b, total):
            choose = pick[b]
            weight = jnp.exp(max_buf[b] - dot(choose, highest)) * total_buf[b]
            for h in range(heads):
                cols = slice(h * HEAD_SIZE, (h + 1) * HEAD_SIZE)
                unit_buf[b, :, cols] = (unit_buf[b, :, cols].astype(F32) * weight[:, h : h + 1]).astype(BF16)
            top, rest = split_total(weight)
            return total + lax.dot_general(
                choose,
                top.astype(BF16),
                (((0,), (0,)), ((), ())),
                preferred_element_type=F32,
            ) + lax.dot_general(
                choose,
                rest.astype(BF16),
                (((0,), (0,)), ((), ())),
                preferred_element_type=F32,
            )

        total = lax.fori_loop(0, blocks, weigh_block, jnp.zeros((all_leaves, HEAD_SIZE), F32))
        for g in range(sg):
            cols = slice(g * PER_GROUP * HEAD_SIZE, (g + 1) * PER_GROUP * HEAD_SIZE)
            num = dot(pick_t[...], unit_buf[:, :, cols].reshape(blocks * cap, PER_GROUP * HEAD_SIZE))
            part[s, :, :, cols] = num.astype(BF16).reshape(n, leaves, PER_GROUP * HEAD_SIZE)
        part[s, :, :, width:] = pack_stats(highest.astype(F32), total).reshape(n, leaves, HEAD_SIZE)

    def y_copy(s, zz):
        return pltpu.make_async_remote_copy(
            src_ref=part.at[s, zz * ROW_PAIR + other_y],
            dst_ref=y_recv.at[s, zz],
            send_sem=y_send_sem.at[s, zz],
            recv_sem=y_recv_sem.at[s, zz],
            device_id=where_is(z, other_y),
            device_id_type=MESH,
        )

    def y_start(s):
        for d in range(1, nz + 1):
            y_copy(s, (z + d) % nz).start()

    def z_copy(s, zz, slot):
        return pltpu.make_async_remote_copy(
            src_ref=merged.at[s, zz],
            dst_ref=z_recv.at[s, slot],
            send_sem=z_send_sem.at[s, zz],
            recv_sem=z_recv_sem.at[s, slot],
            device_id=where_is(zz, y),
            device_id_type=MESH,
        )

    def z_start(s):
        for d in range(1, nz + 1):
            zz = (z + d) % nz
            y_copy(s, zz).wait_recv()
            mine = zz * ROW_PAIR + y
            ref_a, tot_a = unpack_stats(part[s, mine, :, width:])
            ref_b, tot_b = unpack_stats(y_recv[s, zz, :, width:])
            ref = jnp.maximum(ref_a, ref_b)
            ea = jnp.exp(ref_a - ref)
            eb = jnp.exp(ref_b - ref)
            for h in range(heads):
                cols = slice(h * HEAD_SIZE, (h + 1) * HEAD_SIZE)
                merged[s, zz, :, cols] = (
                    part[s, mine, :, cols].astype(F32) * ea[:, h : h + 1]
                    + y_recv[s, zz, :, cols].astype(F32) * eb[:, h : h + 1]
                ).astype(BF16)
            merged[s, zz, :, width:] = pack_stats(ref, ea * tot_a + eb * tot_b)
            if d < nz:
                z_copy(s, zz, z).start()

    lane_leaf = lax.broadcasted_iota(jnp.int32, (leaves, HEAD_SIZE), 1)

    def finish(s):
        own = jnp.zeros((leaves, HEAD_SIZE), F32)
        for h in range(heads):
            at = (s * heads + h) * HEAD_SIZE
            kat = (s * sg + h // PER_GROUP) * HEAD_SIZE
            score = jnp.sum(
                q_ref[:, at : at + HEAD_SIZE].astype(F32) * nk_ref[:, kat : kat + HEAD_SIZE].astype(F32),
                axis=1,
                keepdims=True,
            )
            own = jnp.where(lane_leaf == h, score * scale, own)
        for d in range(1, nz):
            zz = (z + d) % nz
            z_copy(s, zz, zz).wait_recv()
        pieces = [(merged, z)] + [(z_recv, (z + d) % nz) for d in range(1, nz)]
        stats = [unpack_stats(buf[s, idx, :, width:]) for buf, idx in pieces]
        top = own
        for ref, _ in stats:
            top = jnp.maximum(top, ref)
        own_weight = jnp.exp(own - top)
        factors = [jnp.exp(ref - top) for ref, _ in stats]
        below = own_weight
        for factor, (_, tot) in zip(factors, stats):
            below = below + factor * tot
        inverse = 1.0 / below
        own_weight = own_weight * inverse
        factors = [factor * inverse for factor in factors]
        for h in range(heads):
            cols = slice(h * HEAD_SIZE, (h + 1) * HEAD_SIZE)
            kat = (s * sg + h // PER_GROUP) * HEAD_SIZE
            acc = own_weight[:, h : h + 1] * nv_ref[:, kat : kat + HEAD_SIZE].astype(F32)
            for factor, (buf, idx) in zip(factors, pieces):
                acc = acc + factor[:, h : h + 1] * buf[s, idx, :, cols].astype(F32)
            att_buf[s, me, :, cols] = acc.astype(BF16)

    for s in range(slices):
        if s > 0:
            for d in range(1, nz):
                gather_step(q_buf, s, q_row + s, d)
        gather_finish(q_buf, s, q_row + s)
        attend(s)
        y_start(s)
        if s >= 1:
            z_start(s - 1)
        if s >= 2:
            finish(s - 2)
            gather_start(att_buf, s - 2, a_row + s - 2)
    z_start(slices - 1)
    for s in range(max(slices - 2, 0), slices):
        finish(s)
        gather_start(att_buf, s, a_row + s)
    for s in range(slices):
        for d in range(1, nz):
            gather_step(att_buf, s, a_row + s, d)
    weight_copy.wait()
    half = n // 2
    rows = half * leaves
    for s in range(slices):
        gather_finish(att_buf, s, a_row + s)

    def project(start):
        acc = None
        for s in range(slices):
            piece = dot(
                att_buf[s, pl.ds(start, half)].reshape(rows, width),
                weight_buf[s * width : (s + 1) * width, :],
            )
            acc = piece if acc is None else acc + piece
        return acc

    half_send[...] = project((1 - core) * half)
    half_copy = pltpu.make_async_remote_copy(
        src_ref=half_send,
        dst_ref=half_recv,
        send_sem=h_send_sem,
        recv_sem=h_recv_sem,
        device_id=(parts_at, me, 1 - core),
        device_id_type=MESH,
    )
    half_copy.start()
    kept = project(core * half)

    gather_drain(info_buf, 0, 0)
    for s in range(slices):
        gather_drain(q_buf, s, q_row + s)
        gather_drain(att_buf, s, a_row + s)
        for d in range(1, nz + 1):
            y_copy(s, (z + d) % nz).wait_send()
        for d in range(1, nz):
            z_copy(s, (z + d) % nz, z).wait_send()
    half_copy.wait()
    out_ref[...] = (kept + half_recv[...]).astype(BF16)


def local(
    queries,
    block_key_cache,
    block_value_cache,
    new_keys,
    leaf_value_rows,
    ancestors,
    block_slot,
    last_len,
    o_weight,
):
    n = lax.axis_size("blk")
    leaves, features = queries.shape
    ancestry = ancestors.shape[1]
    blocks, block_len, kv_width = block_key_cache.shape
    block_count = blocks * n
    cap = 2 * leaves * ancestry // block_count * n
    slices = SLICES
    nz = n // ROW_PAIR
    heads = kv_width // HEAD_SIZE // slices * PER_GROUP
    width = heads * HEAD_SIZE
    packed = width + HEAD_SIZE
    columns = o_weight.shape[1]

    catalog = jnp.arange(block_count, dtype=jnp.int32)
    slot = jnp.sum(
        jnp.where(ancestors[:, :, None] == catalog, block_slot[None, None, :], 0), axis=2
    )
    low = jnp.minimum(last_len, 256)
    info = jnp.concatenate(
        [slot, low[:, None], (last_len - low)[:, None]], axis=1
    ).astype(BF16)
    info = jnp.pad(info, ((0, 0), (0, HEAD_SIZE - ancestry - 2)))

    vmem = pl.BlockSpec(memory_space=pltpu.VMEM)
    anywhere = pl.BlockSpec(memory_space=pl.ANY)
    dma = pltpu.SemaphoreType.DMA
    grows = 1 + 2 * slices
    return pl.pallas_call(
        functools.partial(kernel, n, slices, cap),
        out_shape=jax.ShapeDtypeStruct((n * leaves // 2, columns), BF16),
        in_specs=[vmem] * 4 + [anywhere] * 3,
        out_specs=vmem,
        scratch_shapes=[
            pltpu.VMEM((1, n, leaves, HEAD_SIZE), BF16),
            pltpu.VMEM((slices, n, leaves, width), BF16),
            pltpu.VMEM((blocks, block_len, kv_width), BF16),
            pltpu.VMEM((blocks, block_len, kv_width), BF16),
            pltpu.VMEM(o_weight.shape, BF16),
            pltpu.VMEM((blocks, cap, n * leaves), BF16),
            pltpu.VMEM((n * leaves, blocks * cap), BF16),
            pltpu.VMEM((blocks, cap, HEAD_SIZE), F32),
            pltpu.VMEM((blocks, cap, width), BF16),
            pltpu.VMEM((blocks, cap, HEAD_SIZE), F32),
            pltpu.VMEM((blocks, cap, HEAD_SIZE), F32),
            pltpu.VMEM((slices, n, leaves, packed), BF16),
            pltpu.VMEM((slices, nz, leaves, packed), BF16),
            pltpu.VMEM((slices, nz, leaves, packed), BF16),
            pltpu.VMEM((slices, nz, leaves, packed), BF16),
            pltpu.VMEM((slices, n, leaves, width), BF16),
            pltpu.VMEM((n * leaves // 2, columns), F32),
            pltpu.VMEM((n * leaves // 2, columns), F32),
            dma((2, blocks)),
            dma,
            dma((grows, n)),
            dma((grows, nz)),
            dma((grows, nz)),
            dma((grows, nz)),
            dma((slices, nz)),
            dma((slices, nz)),
            dma((slices, nz)),
            dma((slices, nz)),
            dma,
            dma,
        ],
        compiler_params=pltpu.CompilerParams(
            collective_id=0, has_side_effects=True, vmem_limit_bytes=56 * 1024 * 1024
        ),
        cost_estimate=pl.CostEstimate(
            flops=4_000_000_000, bytes_accessed=12_000_000, transcendentals=5_000_000
        ),
    )(
        queries,
        info,
        new_keys,
        leaf_value_rows,
        block_key_cache,
        block_value_cache,
        o_weight,
    )


def solution(mesh):
    return jax.shard_map(
        local,
        mesh=mesh,
        in_specs=(
            P(("parts", "blk"), "kvh"),
            P(("parts", "blk"), None, "kvh"),
            P(("parts", "blk"), None, "kvh"),
            P(("parts", "blk"), "kvh"),
            P(("parts", "blk"), "kvh"),
            P(("parts", "blk"), None),
            P("parts"),
            P(("parts", "blk")),
            P("kvh", "blk"),
        ),
        out_specs=P(("parts", "kvh"), "blk"),
        check_vma=False,
    )
```

```python
import functools
import math

import jax
import jax.numpy as jnp
from jax import lax
from jax.experimental import pallas as pl
from jax.experimental.pallas import tpu as pltpu
from jax.sharding import PartitionSpec as P

QUERY_HEADS = 40
KEY_VALUE_HEADS = 8
HEAD_SIZE = 128
PER_GROUP = QUERY_HEADS // KEY_VALUE_HEADS
ROW_PAIR = 2
SLICES = 2
UNROLL = 8
NEG = -1e30
MESH = pl.DeviceIdType.MESH
F32 = jnp.float32
BF16 = jnp.bfloat16


def dot(a, b):
    return jnp.dot(a, b, preferred_element_type=F32)


def kernel(
    n,
    slices,
    cap,
    q_ref,
    path_ref,
    last_ref,
    slot_ref,
    nk_ref,
    nv_ref,
    key_hbm,
    value_hbm,
    weight_hbm,
    out_ref,
    info_buf,
    q_buf,
    key_buf,
    value_buf,
    weight_buf,
    pick,
    pick_t,
    pick_m,
    count,
    unit_buf,
    max_buf,
    total_buf,
    part,
    y_recv,
    merged,
    z_recv,
    att_buf,
    half_send,
    half_keep,
    half_recv,
    kv_sem,
    w_sem,
    g_recv,
    g_up,
    g_down,
    g_side,
    y_send_sem,
    y_recv_sem,
    z_send_sem,
    z_recv_sem,
    h_send_sem,
    h_recv_sem,
):
    parts_at = lax.axis_index("parts")
    me = lax.axis_index("blk")
    core = lax.axis_index("kvh")
    nz = n // ROW_PAIR
    z = me // ROW_PAIR
    y = me % ROW_PAIR
    other_y = 1 - y
    leaves = q_ref.shape[0]
    all_leaves = n * leaves
    blocks, block_len, kv_width = key_hbm.shape
    groups = kv_width // HEAD_SIZE
    sg = groups // slices
    heads = sg * PER_GROUP
    width = heads * HEAD_SIZE
    scale = 1.0 / math.sqrt(HEAD_SIZE)
    scale2 = scale * math.log2(math.e)

    def where_is(zz, yy):
        return (parts_at, zz * ROW_PAIR + yy, core)

    kv_copies = []
    for b in range(blocks):
        kv_copies.append(
            (
                pltpu.make_async_copy(key_hbm.at[b], key_buf.at[b], kv_sem.at[0, b]),
                pltpu.make_async_copy(value_hbm.at[b], value_buf.at[b], kv_sem.at[1, b]),
            )
        )

    info_buf[0, me] = jnp.zeros((16, HEAD_SIZE), jnp.int32)
    info_buf[0, me, 0:8, 0:leaves] = path_ref[...]
    info_buf[0, me, 8:9, 0:leaves] = last_ref[...]
    for s in range(slices):
        q_buf[s, me] = q_ref[:, s * width : (s + 1) * width]

    barrier = pltpu.get_barrier_semaphore()
    for d in range(1, nz):
        pl.semaphore_signal(
            barrier, inc=1, device_id=where_is((z + d) % nz, y), device_id_type=MESH
        )
    pl.semaphore_signal(barrier, inc=1, device_id=where_is(z, other_y), device_id_type=MESH)
    pl.semaphore_signal(barrier, inc=1, device_id=(parts_at, me, 1 - core), device_id_type=MESH)
    pl.semaphore_wait(barrier, nz + 1)

    def gather_copy(buf, s, row, zz, yy, target, send_sem):
        idx = zz * ROW_PAIR + yy
        return pltpu.make_async_remote_copy(
            src_ref=buf.at[s, idx],
            dst_ref=buf.at[s, idx],
            send_sem=send_sem.at[row, zz],
            recv_sem=g_recv.at[row, idx],
            device_id=target,
            device_id_type=MESH,
        )

    def up_copy(buf, s, row, zz):
        return gather_copy(buf, s, row, zz, y, where_is(jnp.minimum(z + 1, nz - 1), y), g_up)

    def down_copy(buf, s, row, zz):
        return gather_copy(buf, s, row, zz, y, where_is(jnp.maximum(z - 1, 0), y), g_down)

    def side_copy(buf, s, row, zz, yy):
        return gather_copy(buf, s, row, zz, yy, where_is(z, other_y), g_side)

    def gather_start(buf, s, row):
        @pl.when(z < nz - 1)
        def _():
            up_copy(buf, s, row, z).start()

        @pl.when(z > 0)
        def _():
            down_copy(buf, s, row, z).start()

        side_copy(buf, s, row, z, y).start()

    def gather_step(buf, s, row, d):
        @pl.when(z - d >= 0)
        def _():
            zz = z - d
            side_copy(buf, s, row, zz, y).wait_recv()

            @pl.when(z < nz - 1)
            def _():
                up_copy(buf, s, row, zz).start()

            side_copy(buf, s, row, zz, y).start()

        @pl.when(z + d < nz)
        def _():
            zz = z + d
            side_copy(buf, s, row, zz, y).wait_recv()

            @pl.when(z > 0)
            def _():
                down_copy(buf, s, row, zz).start()

            side_copy(buf, s, row, zz, y).start()

    def gather_finish(buf, s, row):
        for zz in range(nz):
            side_copy(buf, s, row, zz, other_y).wait_recv()

    def gather_drain(buf, s, row):
        for zz in range(nz):
            side_copy(buf, s, row, zz, y).wait_send()

            @pl.when((zz <= z) & (z < nz - 1))
            def _():
                up_copy(buf, s, row, zz).wait_send()

            @pl.when((zz >= z) & (z > 0))
            def _():
                down_copy(buf, s, row, zz).wait_send()

    q_row = 1
    a_row = 1 + slices

    def query_wave(w):
        if w < slices:
            gather_start(q_buf, w, q_row + w)
        for s in range(slices):
            if 1 <= w - s < nz:
                gather_step(q_buf, s, q_row + s, w - s)

    gather_start(info_buf, 0, 0)
    query_wave(0)
    for b in range(blocks):
        kv_copies[b][0].start()
        kv_copies[b][1].start()
    weight_copy = pltpu.make_async_copy(weight_hbm, weight_buf, w_sem)
    weight_copy.start()
    for d in range(1, nz):
        gather_step(info_buf, 0, 0, d)
        query_wave(d)
    gather_finish(info_buf, 0, 0)

    info_t = jnp.concatenate([info_buf[0, i, :, 0:leaves] for i in range(n)], axis=1)
    path = info_t[0:8]
    last = info_t[8:9].astype(F32)
    level = lax.broadcasted_iota(jnp.int32, (8, all_leaves), 0)
    lengths = jnp.where(level == 7, last, float(block_len))
    slot_of = slot_ref[...]
    block_id = lax.broadcasted_iota(jnp.int32, slot_of.shape, 1)
    first = lax.broadcasted_iota(jnp.int32, (8, all_leaves), 0)
    present = jnp.zeros((8, all_leaves), F32)
    valid = jnp.zeros((8, all_leaves), F32)
    for b in range(blocks):
        mine = jnp.sum(jnp.where(slot_of == me * blocks + b, block_id, 0), axis=1, keepdims=True)
        same = path == mine
        here = jnp.sum(jnp.where(same, 1.0, 0.0), axis=0, keepdims=True)
        size = jnp.sum(jnp.where(same, lengths, 0.0), axis=0, keepdims=True)
        present = jnp.where(first == b, here, present)
        valid = jnp.where(first == b, size, valid)
    earlier = (
        lax.broadcasted_iota(jnp.int32, (all_leaves, all_leaves), 0)
        < lax.broadcasted_iota(jnp.int32, (all_leaves, all_leaves), 1)
    )
    rank = dot(present.astype(BF16), jnp.where(earlier, 1.0, 0.0).astype(BF16))
    rank = jnp.where(present > 0.5, rank, -1.0)
    ordinal = lax.broadcasted_iota(jnp.int32, (cap, all_leaves), 0).astype(F32)
    for b in range(blocks):
        chosen = jnp.where(ordinal == rank[b : b + 1], 1.0, 0.0)
        count[b] = jnp.broadcast_to(
            jnp.sum(chosen * valid[b : b + 1], axis=1, keepdims=True), (cap, HEAD_SIZE)
        )
        pick[b] = chosen.astype(BF16)
        back = jnp.transpose(chosen)
        pick_t[:, b * cap : (b + 1) * cap] = back.astype(BF16)
        missing = 1.0 - jnp.sum(back, axis=1, keepdims=True)
        spot = lax.broadcasted_iota(jnp.int32, (all_leaves, HEAD_SIZE - cap), 1)
        pick_m[b] = jnp.concatenate([back, jnp.where(spot == 0, missing, 0.0)], axis=1).astype(BF16)

    lane_cap = lax.broadcasted_iota(jnp.int32, (cap, HEAD_SIZE), 1)
    position = lax.broadcasted_iota(jnp.int32, (PER_GROUP * cap, block_len), 1).astype(F32)
    ones = jnp.ones((block_len, HEAD_SIZE), BF16)
    floor_rows = jnp.where(
        lax.broadcasted_iota(jnp.int32, (HEAD_SIZE - cap, HEAD_SIZE), 0) == 0, NEG, 0.0
    ).astype(BF16)

    def split_total(value):
        top = value.astype(BF16).astype(F32)
        return top, (value - top).astype(BF16).astype(F32)

    def pack_stats(reference, total):
        top, rest = split_total(total)
        lane = lax.broadcasted_iota(jnp.int32, reference.shape, 1)
        return jnp.where(
            lane < 32,
            reference,
            jnp.where(lane < 64, pltpu.roll(top, 32, 1), pltpu.roll(rest, 64, 1)),
        ).astype(BF16)

    def unpack_stats(stats):
        stats = stats.astype(F32)
        return stats, pltpu.roll(stats, 96, 1) + pltpu.roll(stats, 64, 1)

    def score(s):
        if s == 0:
            for b in range(blocks):
                kv_copies[b][0].wait()
                kv_copies[b][1].wait()

        def score_block(b, highest):
            choose = pick[b]
            rows = dot(choose, q_buf[s].reshape(all_leaves, width)).astype(BF16)
            limit = count[b][:, 0:1]
            limit = jnp.concatenate([limit] * PER_GROUP, axis=0)
            inside = position < limit
            max_here = jnp.zeros((cap, HEAD_SIZE), F32)
            total_here = jnp.zeros((cap, HEAD_SIZE), F32)
            for g in range(sg):
                at = (s * sg + g) * HEAD_SIZE
                group_rows = jnp.concatenate(
                    [
                        rows[:, (g * PER_GROUP + e) * HEAD_SIZE : (g * PER_GROUP + e + 1) * HEAD_SIZE]
                        for e in range(PER_GROUP)
                    ],
                    axis=0,
                )
                scores = lax.dot_general(
                    group_rows,
                    key_buf[b, :, at : at + HEAD_SIZE],
                    (((1,), (1,)), ((), ())),
                    preferred_element_type=F32,
                )
                scores = jnp.where(inside, scores, NEG)
                top = jnp.max(scores, axis=1, keepdims=True)
                shares = jnp.exp2((scores - top) * scale2).astype(BF16)
                both = dot(
                    shares,
                    jnp.concatenate([value_buf[b, :, at : at + HEAD_SIZE], ones], axis=1),
                )
                sums = both[:, HEAD_SIZE:]
                unit = (both[:, :HEAD_SIZE] / sums).astype(BF16)
                scaled_top = top * scale
                for e in range(PER_GROUP):
                    h = g * PER_GROUP + e
                    unit_buf[b, :, h * HEAD_SIZE : (h + 1) * HEAD_SIZE] = unit[e * cap : (e + 1) * cap]
                    max_here = jnp.where(lane_cap == h, scaled_top[e * cap : (e + 1) * cap], max_here)
                    total_here = jnp.where(lane_cap == h, sums[e * cap : (e + 1) * cap], total_here)
            max_buf[b] = max_here
            total_buf[b] = total_here
            spread = dot(pick_m[b], jnp.concatenate([max_here.astype(BF16), floor_rows], axis=0))
            return jnp.maximum(highest, spread)

        highest = lax.fori_loop(
            0, blocks, score_block, jnp.full((all_leaves, HEAD_SIZE), NEG, F32), unroll=UNROLL
        )
        return highest.astype(BF16)

    def weigh(s, highest):
        def weigh_block(b, carry):
            weight = jnp.exp(max_buf[b] - dot(pick[b], highest)) * total_buf[b]
            for h in range(heads):
                cols = slice(h * HEAD_SIZE, (h + 1) * HEAD_SIZE)
                unit_buf[b, :, cols] = (unit_buf[b, :, cols].astype(F32) * weight[:, h : h + 1]).astype(BF16)
            top, rest = split_total(weight)
            unit_buf[b, :, width : width + HEAD_SIZE] = top.astype(BF16)
            unit_buf[b, :, width + HEAD_SIZE :] = rest.astype(BF16)
            return carry

        lax.fori_loop(0, blocks, weigh_block, 0, unroll=UNROLL)
        for g in range(sg):
            cols = slice(g * PER_GROUP * HEAD_SIZE, (g + 1) * PER_GROUP * HEAD_SIZE)
            num = dot(pick_t[...], unit_buf[:, :, cols].reshape(blocks * cap, PER_GROUP * HEAD_SIZE))
            part[s, :, :, cols] = num.astype(BF16).reshape(n, leaves, PER_GROUP * HEAD_SIZE)
        total = dot(pick_t[...], unit_buf[:, :, width:].reshape(blocks * cap, 2 * HEAD_SIZE))
        total = total[:, :HEAD_SIZE] + total[:, HEAD_SIZE:]
        part[s, :, :, width:] = pack_stats(highest.astype(F32), total).reshape(n, leaves, HEAD_SIZE)

    def y_copy(s, zz):
        return pltpu.make_async_remote_copy(
            src_ref=part.at[s, zz * ROW_PAIR + other_y],
            dst_ref=y_recv.at[s, zz],
            send_sem=y_send_sem.at[s, zz],
            recv_sem=y_recv_sem.at[s, zz],
            device_id=where_is(z, other_y),
            device_id_type=MESH,
        )

    def y_start(s):
        for d in range(1, nz + 1):
            y_copy(s, (z + d) % nz).start()

    def z_copy(s, zz, slot):
        return pltpu.make_async_remote_copy(
            src_ref=merged.at[s, zz],
            dst_ref=z_recv.at[s, slot],
            send_sem=z_send_sem.at[s, zz],
            recv_sem=z_recv_sem.at[s, slot],
            device_id=where_is(zz, y),
            device_id_type=MESH,
        )

    def z_start(s):
        for d in range(1, nz + 1):
            zz = (z + d) % nz
            y_copy(s, zz).wait_recv()
            mine = zz * ROW_PAIR + y
            ref_a, tot_a = unpack_stats(part[s, mine, :, width:])
            ref_b, tot_b = unpack_stats(y_recv[s, zz, :, width:])
            ref = jnp.maximum(ref_a, ref_b)
            ea = jnp.exp(ref_a - ref)
            eb = jnp.exp(ref_b - ref)
            for h in range(heads):
                cols = slice(h * HEAD_SIZE, (h + 1) * HEAD_SIZE)
                merged[s, zz, :, cols] = (
                    part[s, mine, :, cols].astype(F32) * ea[:, h : h + 1]
                    + y_recv[s, zz, :, cols].astype(F32) * eb[:, h : h + 1]
                ).astype(BF16)
            merged[s, zz, :, width:] = pack_stats(ref, ea * tot_a + eb * tot_b)
            if d < nz:
                z_copy(s, zz, z).start()

    lane_leaf = lax.broadcasted_iota(jnp.int32, (leaves, HEAD_SIZE), 1)

    def finish(s):
        own = jnp.zeros((leaves, HEAD_SIZE), F32)
        for h in range(heads):
            at = (s * heads + h) * HEAD_SIZE
            kat = (s * sg + h // PER_GROUP) * HEAD_SIZE
            score = jnp.sum(
                q_ref[:, at : at + HEAD_SIZE].astype(F32) * nk_ref[:, kat : kat + HEAD_SIZE].astype(F32),
                axis=1,
                keepdims=True,
            )
            own = jnp.where(lane_leaf == h, score * scale, own)
        for d in range(1, nz):
            zz = (z + d) % nz
            z_copy(s, zz, zz).wait_recv()
        pieces = [(merged, z)] + [(z_recv, (z + d) % nz) for d in range(1, nz)]
        stats = [unpack_stats(buf[s, idx, :, width:]) for buf, idx in pieces]
        top = own
        for ref, _ in stats:
            top = jnp.maximum(top, ref)
        own_weight = jnp.exp(own - top)
        factors = [jnp.exp(ref - top) for ref, _ in stats]
        below = own_weight
        for factor, (_, tot) in zip(factors, stats):
            below = below + factor * tot
        inverse = 1.0 / below
        own_weight = own_weight * inverse
        factors = [factor * inverse for factor in factors]
        for h in range(heads):
            cols = slice(h * HEAD_SIZE, (h + 1) * HEAD_SIZE)
            kat = (s * sg + h // PER_GROUP) * HEAD_SIZE
            acc = own_weight[:, h : h + 1] * nv_ref[:, kat : kat + HEAD_SIZE].astype(F32)
            for factor, (buf, idx) in zip(factors, pieces):
                acc = acc + factor[:, h : h + 1] * buf[s, idx, :, cols].astype(F32)
            att_buf[s, me, :, cols] = acc.astype(BF16)

    half = n // 2
    rows = half * leaves
    end = slices - 1

    def att_wave(w):
        if w < slices:
            finish(w)
            gather_start(att_buf, w, a_row + w)
        for s in range(slices):
            if 1 <= w - s < nz:
                gather_step(att_buf, s, a_row + s, w - s)

    def project(s, start):
        return dot(
            att_buf[s, pl.ds(start, half)].reshape(rows, width),
            weight_buf[s * width : (s + 1) * width, :],
        )

    def project_both(s):
        gather_finish(att_buf, s, a_row + s)
        sent = project(s, (1 - core) * half)
        own = project(s, core * half)
        half_send[...] = sent if s == 0 else half_send[...] + sent
        half_keep[...] = own if s == 0 else half_keep[...] + own

    wave = nz
    query_wave(wave)
    for s in range(slices):
        if s == slices - 1:
            for w in range(wave + 1, slices + nz - 1):
                query_wave(w)
        gather_finish(q_buf, s, q_row + s)
        highest = score(s)
        if s < slices - 2:
            wave = wave + 1
            if wave < slices + nz - 1:
                query_wave(wave)
        if s >= 2:
            att_wave(s - 2)
        if s >= 1:
            z_start(s - 1)
        weigh(s, highest)
        y_start(s)
    weight_copy.wait()
    for w in range(max(slices - 2, 0), end):
        att_wave(w)
    z_start(end)
    for w in range(end, slices + nz - 1):
        att_wave(w)
        if 0 <= w - nz < end:
            project_both(w - nz)
    gather_finish(att_buf, end, a_row + end)
    sent = project(end, (1 - core) * half)
    half_send[...] = sent if end == 0 else half_send[...] + sent
    half_copy = pltpu.make_async_remote_copy(
        src_ref=half_send,
        dst_ref=half_recv,
        send_sem=h_send_sem,
        recv_sem=h_recv_sem,
        device_id=(parts_at, me, 1 - core),
        device_id_type=MESH,
    )
    half_copy.start()
    kept = project(end, core * half)
    if end > 0:
        kept = kept + half_keep[...]

    gather_drain(info_buf, 0, 0)
    for s in range(slices):
        gather_drain(q_buf, s, q_row + s)
        gather_drain(att_buf, s, a_row + s)
        for d in range(1, nz + 1):
            y_copy(s, (z + d) % nz).wait_send()
        for d in range(1, nz):
            z_copy(s, (z + d) % nz, z).wait_send()
    half_copy.wait()
    out_ref[...] = (kept + half_recv[...]).astype(BF16)


def local(
    queries,
    block_key_cache,
    block_value_cache,
    new_keys,
    leaf_value_rows,
    ancestors,
    block_slot,
    last_len,
    o_weight,
):
    n = lax.axis_size("blk")
    leaves, features = queries.shape
    ancestry = ancestors.shape[1]
    blocks, block_len, kv_width = block_key_cache.shape
    block_count = blocks * n
    cap = 2 * leaves * ancestry // block_count * n
    slices = SLICES
    nz = n // ROW_PAIR
    heads = kv_width // HEAD_SIZE // slices * PER_GROUP
    width = heads * HEAD_SIZE
    packed = width + HEAD_SIZE
    columns = o_weight.shape[1]

    vmem = pl.BlockSpec(memory_space=pltpu.VMEM)
    anywhere = pl.BlockSpec(memory_space=pl.ANY)
    dma = pltpu.SemaphoreType.DMA
    grows = 1 + 2 * slices
    return pl.pallas_call(
        functools.partial(kernel, n, slices, cap),
        out_shape=jax.ShapeDtypeStruct((n * leaves // 2, columns), BF16),
        in_specs=[vmem] * 6 + [anywhere] * 3,
        out_specs=vmem,
        scratch_shapes=[
            pltpu.VMEM((1, n, 16, HEAD_SIZE), jnp.int32),
            pltpu.VMEM((slices, n, leaves, width), BF16),
            pltpu.VMEM((blocks, block_len, kv_width), BF16),
            pltpu.VMEM((blocks, block_len, kv_width), BF16),
            pltpu.VMEM(o_weight.shape, BF16),
            pltpu.VMEM((blocks, cap, n * leaves), BF16),
            pltpu.VMEM((n * leaves, blocks * cap), BF16),
            pltpu.VMEM((blocks, n * leaves, HEAD_SIZE), BF16),
            pltpu.VMEM((blocks, cap, HEAD_SIZE), F32),
            pltpu.VMEM((blocks, cap, width + 2 * HEAD_SIZE), BF16),
            pltpu.VMEM((blocks, cap, HEAD_SIZE), F32),
            pltpu.VMEM((blocks, cap, HEAD_SIZE), F32),
            pltpu.VMEM((slices, n, leaves, packed), BF16),
            pltpu.VMEM((slices, nz, leaves, packed), BF16),
            pltpu.VMEM((slices, nz, leaves, packed), BF16),
            pltpu.VMEM((slices, nz, leaves, packed), BF16),
            pltpu.VMEM((slices, n, leaves, width), BF16),
            pltpu.VMEM((n * leaves // 2, columns), F32),
            pltpu.VMEM((n * leaves // 2, columns), F32),
            pltpu.VMEM((n * leaves // 2, columns), F32),
            dma((2, blocks)),
            dma,
            dma((grows, n)),
            dma((grows, nz)),
            dma((grows, nz)),
            dma((grows, nz)),
            dma((slices, nz)),
            dma((slices, nz)),
            dma((slices, nz)),
            dma((slices, nz)),
            dma,
            dma,
        ],
        compiler_params=pltpu.CompilerParams(
            collective_id=0, has_side_effects=True, vmem_limit_bytes=56 * 1024 * 1024
        ),
        cost_estimate=pl.CostEstimate(
            flops=4_000_000_000, bytes_accessed=12_000_000, transcendentals=5_000_000
        ),
    )(
        queries,
        ancestors.T,
        last_len[None, :],
        block_slot[None, :],
        new_keys,
        leaf_value_rows,
        block_key_cache,
        block_value_cache,
        o_weight,
    )


def solution(mesh):
    return jax.shard_map(
        local,
        mesh=mesh,
        in_specs=(
            P(("parts", "blk"), "kvh"),
            P(("parts", "blk"), None, "kvh"),
            P(("parts", "blk"), None, "kvh"),
            P(("parts", "blk"), "kvh"),
            P(("parts", "blk"), "kvh"),
            P(("parts", "blk"), None),
            P("parts"),
            P(("parts", "blk")),
            P("kvh", "blk"),
        ),
        out_specs=P(("parts", "kvh"), "blk"),
        check_vma=False,
    )
```

```python
import functools
import math

import jax
import jax.numpy as jnp
from jax import lax
from jax.experimental import pallas as pl
from jax.experimental.pallas import tpu as pltpu
from jax.sharding import PartitionSpec as P

QUERY_HEADS = 40
KEY_VALUE_HEADS = 8
HEAD_SIZE = 128
PER_GROUP = QUERY_HEADS // KEY_VALUE_HEADS
ROW_PAIR = 2
SLICES = 2
UNROLL = 8
NEG = -1e30
MESH = pl.DeviceIdType.MESH
F32 = jnp.float32
BF16 = jnp.bfloat16


def dot(a, b):
    return jnp.dot(a, b, preferred_element_type=F32)


def kernel(
    n,
    slices,
    cap,
    q_ref,
    path_ref,
    last_ref,
    slot_ref,
    nk_ref,
    nv_ref,
    key_hbm,
    value_hbm,
    weight_hbm,
    out_ref,
    info_buf,
    q_buf,
    key_buf,
    value_buf,
    weight_buf,
    pick,
    pick_t,
    pick_m,
    count,
    unit_buf,
    max_buf,
    total_buf,
    part,
    y_recv,
    merged,
    z_recv,
    att_buf,
    half_send,
    half_keep,
    half_recv,
    kv_sem,
    w_sem,
    g_recv,
    g_up,
    g_down,
    g_side,
    y_send_sem,
    y_recv_sem,
    z_send_sem,
    z_recv_sem,
    h_send_sem,
    h_recv_sem,
):
    parts_at = lax.axis_index("parts")
    me = lax.axis_index("blk")
    core = lax.axis_index("kvh")
    nz = n // ROW_PAIR
    z = me // ROW_PAIR
    y = me % ROW_PAIR
    other_y = 1 - y
    leaves = q_ref.shape[0]
    all_leaves = n * leaves
    blocks, block_len, kv_width = key_hbm.shape
    groups = kv_width // HEAD_SIZE
    sg = groups // slices
    heads = sg * PER_GROUP
    width = heads * HEAD_SIZE
    scale = 1.0 / math.sqrt(HEAD_SIZE)
    scale2 = scale * math.log2(math.e)

    def where_is(zz, yy):
        return (parts_at, zz * ROW_PAIR + yy, core)

    kv_copies = []
    for b in range(blocks):
        kv_copies.append(
            (
                pltpu.make_async_copy(key_hbm.at[b], key_buf.at[b], kv_sem.at[0, b]),
                pltpu.make_async_copy(value_hbm.at[b], value_buf.at[b], kv_sem.at[1, b]),
            )
        )

    info_buf[0, me] = jnp.zeros((16, HEAD_SIZE), jnp.int32)
    info_buf[0, me, 0:8, 0:leaves] = path_ref[...]
    info_buf[0, me, 8:9, 0:leaves] = last_ref[...]
    for s in range(slices):
        q_buf[s, me] = q_ref[:, s * width : (s + 1) * width]

    barrier = pltpu.get_barrier_semaphore()
    for d in range(1, nz):
        pl.semaphore_signal(
            barrier, inc=1, device_id=where_is((z + d) % nz, y), device_id_type=MESH
        )
    pl.semaphore_signal(barrier, inc=1, device_id=where_is(z, other_y), device_id_type=MESH)
    pl.semaphore_signal(barrier, inc=1, device_id=(parts_at, me, 1 - core), device_id_type=MESH)
    pl.semaphore_wait(barrier, nz + 1)

    def gather_copy(buf, s, row, zz, yy, target, send_sem):
        idx = zz * ROW_PAIR + yy
        return pltpu.make_async_remote_copy(
            src_ref=buf.at[s, idx],
            dst_ref=buf.at[s, idx],
            send_sem=send_sem.at[row, zz],
            recv_sem=g_recv.at[row, idx],
            device_id=target,
            device_id_type=MESH,
        )

    def up_copy(buf, s, row, zz):
        return gather_copy(buf, s, row, zz, y, where_is(jnp.minimum(z + 1, nz - 1), y), g_up)

    def down_copy(buf, s, row, zz):
        return gather_copy(buf, s, row, zz, y, where_is(jnp.maximum(z - 1, 0), y), g_down)

    def side_copy(buf, s, row, zz, yy):
        return gather_copy(buf, s, row, zz, yy, where_is(z, other_y), g_side)

    def gather_start(buf, s, row):
        @pl.when(z < nz - 1)
        def _():
            up_copy(buf, s, row, z).start()

        @pl.when(z > 0)
        def _():
            down_copy(buf, s, row, z).start()

        side_copy(buf, s, row, z, y).start()

    def gather_step(buf, s, row, d):
        @pl.when(z - d >= 0)
        def _():
            zz = z - d
            side_copy(buf, s, row, zz, y).wait_recv()

            @pl.when(z < nz - 1)
            def _():
                up_copy(buf, s, row, zz).start()

            side_copy(buf, s, row, zz, y).start()

        @pl.when(z + d < nz)
        def _():
            zz = z + d
            side_copy(buf, s, row, zz, y).wait_recv()

            @pl.when(z > 0)
            def _():
                down_copy(buf, s, row, zz).start()

            side_copy(buf, s, row, zz, y).start()

    def gather_finish(buf, s, row):
        for zz in range(nz):
            side_copy(buf, s, row, zz, other_y).wait_recv()

    def gather_drain(buf, s, row):
        for zz in range(nz):
            side_copy(buf, s, row, zz, y).wait_send()

            @pl.when((zz <= z) & (z < nz - 1))
            def _():
                up_copy(buf, s, row, zz).wait_send()

            @pl.when((zz >= z) & (z > 0))
            def _():
                down_copy(buf, s, row, zz).wait_send()

    q_row = 1
    a_row = 1 + slices

    def query_wave(w):
        if w < slices:
            gather_start(q_buf, w, q_row + w)
        for s in range(slices):
            if 1 <= w - s < nz:
                gather_step(q_buf, s, q_row + s, w - s)

    gather_start(info_buf, 0, 0)
    query_wave(0)
    for b in range(blocks):
        kv_copies[b][0].start()
        kv_copies[b][1].start()
    weight_copy = pltpu.make_async_copy(weight_hbm, weight_buf, w_sem)
    weight_copy.start()
    for d in range(1, nz):
        gather_step(info_buf, 0, 0, d)
        query_wave(d)
    gather_finish(info_buf, 0, 0)

    info_t = jnp.concatenate([info_buf[0, i, :, 0:leaves] for i in range(n)], axis=1)
    path = info_t[0:8]
    last = info_t[8:9].astype(F32)
    level = lax.broadcasted_iota(jnp.int32, (8, all_leaves), 0)
    lengths = jnp.where(level == 7, last, float(block_len))
    slot_of = slot_ref[...]
    block_id = lax.broadcasted_iota(jnp.int32, slot_of.shape, 1)
    first = lax.broadcasted_iota(jnp.int32, (8, all_leaves), 0)
    present = jnp.zeros((8, all_leaves), F32)
    valid = jnp.zeros((8, all_leaves), F32)
    for b in range(blocks):
        mine = jnp.sum(jnp.where(slot_of == me * blocks + b, block_id, 0), axis=1, keepdims=True)
        same = path == mine
        here = jnp.sum(jnp.where(same, 1.0, 0.0), axis=0, keepdims=True)
        size = jnp.sum(jnp.where(same, lengths, 0.0), axis=0, keepdims=True)
        present = jnp.where(first == b, here, present)
        valid = jnp.where(first == b, size, valid)
    earlier = (
        lax.broadcasted_iota(jnp.int32, (all_leaves, all_leaves), 0)
        < lax.broadcasted_iota(jnp.int32, (all_leaves, all_leaves), 1)
    )
    rank = dot(present.astype(BF16), jnp.where(earlier, 1.0, 0.0).astype(BF16))
    rank = jnp.where(present > 0.5, rank, -1.0)
    ordinal = lax.broadcasted_iota(jnp.int32, (cap, all_leaves), 0).astype(F32)
    for b in range(blocks):
        chosen = jnp.where(ordinal == rank[b : b + 1], 1.0, 0.0)
        count[b] = jnp.broadcast_to(
            jnp.sum(chosen * valid[b : b + 1], axis=1, keepdims=True), (cap, HEAD_SIZE)
        )
        pick[b] = chosen.astype(BF16)
        back = jnp.transpose(chosen)
        pick_t[:, b * cap : (b + 1) * cap] = back.astype(BF16)
        missing = 1.0 - jnp.sum(back, axis=1, keepdims=True)
        spot = lax.broadcasted_iota(jnp.int32, (all_leaves, HEAD_SIZE - cap), 1)
        pick_m[b] = jnp.concatenate([back, jnp.where(spot == 0, missing, 0.0)], axis=1).astype(BF16)

    lane_cap = lax.broadcasted_iota(jnp.int32, (cap, HEAD_SIZE), 1)
    position = lax.broadcasted_iota(jnp.int32, (PER_GROUP * cap, block_len), 1).astype(F32)
    ones = jnp.ones((block_len, HEAD_SIZE), BF16)
    floor_rows = jnp.where(
        lax.broadcasted_iota(jnp.int32, (HEAD_SIZE - cap, HEAD_SIZE), 0) == 0, NEG, 0.0
    ).astype(BF16)

    def split_total(value):
        top = value.astype(BF16).astype(F32)
        return top, (value - top).astype(BF16).astype(F32)

    def pack_stats(reference, total):
        top, rest = split_total(total)
        lane = lax.broadcasted_iota(jnp.int32, reference.shape, 1)
        return jnp.where(
            lane < 32,
            reference,
            jnp.where(lane < 64, pltpu.roll(top, 32, 1), pltpu.roll(rest, 64, 1)),
        ).astype(BF16)

    def unpack_stats(stats):
        stats = stats.astype(F32)
        return stats, pltpu.roll(stats, 96, 1) + pltpu.roll(stats, 64, 1)

    def score(s):
        if s == 0:
            for b in range(blocks):
                kv_copies[b][0].wait()
                kv_copies[b][1].wait()

        def score_block(b, highest):
            choose = pick[b]
            rows = dot(choose, q_buf[s].reshape(all_leaves, width)).astype(BF16)
            limit = count[b][:, 0:1]
            limit = jnp.concatenate([limit] * PER_GROUP, axis=0)
            inside = position < limit
            max_here = jnp.zeros((cap, HEAD_SIZE), F32)
            total_here = jnp.zeros((cap, HEAD_SIZE), F32)
            for g in range(sg):
                at = (s * sg + g) * HEAD_SIZE
                group_rows = jnp.concatenate(
                    [
                        rows[:, (g * PER_GROUP + e) * HEAD_SIZE : (g * PER_GROUP + e + 1) * HEAD_SIZE]
                        for e in range(PER_GROUP)
                    ],
                    axis=0,
                )
                scores = lax.dot_general(
                    group_rows,
                    key_buf[b, :, at : at + HEAD_SIZE],
                    (((1,), (1,)), ((), ())),
                    preferred_element_type=F32,
                )
                scores = jnp.where(inside, scores, NEG)
                top = jnp.max(scores, axis=1, keepdims=True)
                shares = jnp.exp2((scores - top) * scale2).astype(BF16)
                both = dot(
                    shares,
                    jnp.concatenate([value_buf[b, :, at : at + HEAD_SIZE], ones], axis=1),
                )
                sums = both[:, HEAD_SIZE:]
                unit = (both[:, :HEAD_SIZE] / sums).astype(BF16)
                scaled_top = top * scale
                for e in range(PER_GROUP):
                    h = g * PER_GROUP + e
                    unit_buf[b, :, h * HEAD_SIZE : (h + 1) * HEAD_SIZE] = unit[e * cap : (e + 1) * cap]
                    max_here = jnp.where(lane_cap == h, scaled_top[e * cap : (e + 1) * cap], max_here)
                    total_here = jnp.where(lane_cap == h, sums[e * cap : (e + 1) * cap], total_here)
            max_buf[b] = max_here
            total_buf[b] = total_here
            spread = dot(pick_m[b], jnp.concatenate([max_here.astype(BF16), floor_rows], axis=0))
            return jnp.maximum(highest, spread)

        highest = lax.fori_loop(
            0, blocks, score_block, jnp.full((all_leaves, HEAD_SIZE), NEG, F32), unroll=UNROLL
        )
        return highest.astype(BF16)

    def weigh(s, highest):
        def weigh_block(b, carry):
            weight = jnp.exp(max_buf[b] - dot(pick[b], highest)) * total_buf[b]
            for h in range(heads):
                cols = slice(h * HEAD_SIZE, (h + 1) * HEAD_SIZE)
                unit_buf[b, :, cols] = (unit_buf[b, :, cols].astype(F32) * weight[:, h : h + 1]).astype(BF16)
            top, rest = split_total(weight)
            unit_buf[b, :, width : width + HEAD_SIZE] = top.astype(BF16)
            unit_buf[b, :, width + HEAD_SIZE :] = rest.astype(BF16)
            return carry

        lax.fori_loop(0, blocks, weigh_block, 0, unroll=UNROLL)
        for g in range(sg):
            cols = slice(g * PER_GROUP * HEAD_SIZE, (g + 1) * PER_GROUP * HEAD_SIZE)
            num = dot(pick_t[...], unit_buf[:, :, cols].reshape(blocks * cap, PER_GROUP * HEAD_SIZE))
            part[s, :, :, cols] = num.astype(BF16).reshape(n, leaves, PER_GROUP * HEAD_SIZE)
        total = dot(pick_t[...], unit_buf[:, :, width:].reshape(blocks * cap, 2 * HEAD_SIZE))
        total = total[:, :HEAD_SIZE] + total[:, HEAD_SIZE:]
        part[s, :, :, width:] = pack_stats(highest.astype(F32), total).reshape(n, leaves, HEAD_SIZE)

    def y_copy(s, zz):
        return pltpu.make_async_remote_copy(
            src_ref=part.at[s, zz * ROW_PAIR + other_y],
            dst_ref=y_recv.at[s, zz],
            send_sem=y_send_sem.at[s, zz],
            recv_sem=y_recv_sem.at[s, zz],
            device_id=where_is(z, other_y),
            device_id_type=MESH,
        )

    def y_start(s):
        for d in range(1, nz + 1):
            y_copy(s, (z + d) % nz).start()

    def z_copy(s, zz, slot):
        return pltpu.make_async_remote_copy(
            src_ref=merged.at[s, zz],
            dst_ref=z_recv.at[s, slot],
            send_sem=z_send_sem.at[s, zz],
            recv_sem=z_recv_sem.at[s, slot],
            device_id=where_is(zz, y),
            device_id_type=MESH,
        )

    def z_start(s):
        for d in range(1, nz + 1):
            zz = (z + d) % nz
            y_copy(s, zz).wait_recv()
            mine = zz * ROW_PAIR + y
            ref_a, tot_a = unpack_stats(part[s, mine, :, width:])
            ref_b, tot_b = unpack_stats(y_recv[s, zz, :, width:])
            ref = jnp.maximum(ref_a, ref_b)
            ea = jnp.exp(ref_a - ref)
            eb = jnp.exp(ref_b - ref)
            for h in range(heads):
                cols = slice(h * HEAD_SIZE, (h + 1) * HEAD_SIZE)
                merged[s, zz, :, cols] = (
                    part[s, mine, :, cols].astype(F32) * ea[:, h : h + 1]
                    + y_recv[s, zz, :, cols].astype(F32) * eb[:, h : h + 1]
                ).astype(BF16)
            merged[s, zz, :, width:] = pack_stats(ref, ea * tot_a + eb * tot_b)
            if d < nz:
                z_copy(s, zz, z).start()

    lane_leaf = lax.broadcasted_iota(jnp.int32, (leaves, HEAD_SIZE), 1)

    def finish(s):
        own = jnp.zeros((leaves, HEAD_SIZE), F32)
        for h in range(heads):
            at = (s * heads + h) * HEAD_SIZE
            kat = (s * sg + h // PER_GROUP) * HEAD_SIZE
            score = jnp.sum(
                q_ref[:, at : at + HEAD_SIZE].astype(F32) * nk_ref[:, kat : kat + HEAD_SIZE].astype(F32),
                axis=1,
                keepdims=True,
            )
            own = jnp.where(lane_leaf == h, score * scale, own)
        for d in range(1, nz):
            zz = (z + d) % nz
            z_copy(s, zz, zz).wait_recv()
        pieces = [(merged, z)] + [(z_recv, (z + d) % nz) for d in range(1, nz)]
        stats = [unpack_stats(buf[s, idx, :, width:]) for buf, idx in pieces]
        top = own
        for ref, _ in stats:
            top = jnp.maximum(top, ref)
        own_weight = jnp.exp(own - top)
        factors = [jnp.exp(ref - top) for ref, _ in stats]
        below = own_weight
        for factor, (_, tot) in zip(factors, stats):
            below = below + factor * tot
        inverse = 1.0 / below
        own_weight = own_weight * inverse
        factors = [factor * inverse for factor in factors]
        for h in range(heads):
            cols = slice(h * HEAD_SIZE, (h + 1) * HEAD_SIZE)
            kat = (s * sg + h // PER_GROUP) * HEAD_SIZE
            acc = own_weight[:, h : h + 1] * nv_ref[:, kat : kat + HEAD_SIZE].astype(F32)
            for factor, (buf, idx) in zip(factors, pieces):
                acc = acc + factor[:, h : h + 1] * buf[s, idx, :, cols].astype(F32)
            att_buf[s, me, :, cols] = acc.astype(BF16)

    half = n // 2
    rows = half * leaves
    end = slices - 1

    def att_wave(w):
        if w < slices:
            finish(w)
            gather_start(att_buf, w, a_row + w)
        for s in range(slices):
            if 1 <= w - s < nz:
                gather_step(att_buf, s, a_row + s, w - s)

    def project(s, start):
        return dot(
            att_buf[s, pl.ds(start, half)].reshape(rows, width),
            weight_buf[s * width : (s + 1) * width, :],
        )

    def project_both(s):
        gather_finish(att_buf, s, a_row + s)
        sent = project(s, (1 - core) * half)
        own = project(s, core * half)
        half_send[...] = sent if s == 0 else half_send[...] + sent
        half_keep[...] = own if s == 0 else half_keep[...] + own

    wave = nz
    query_wave(wave)
    for s in range(slices):
        if s == slices - 1:
            for w in range(wave + 1, slices + nz - 1):
                query_wave(w)
        gather_finish(q_buf, s, q_row + s)
        highest = score(s)
        if s < slices - 2:
            wave = wave + 1
            if wave < slices + nz - 1:
                query_wave(wave)
        if s >= 2:
            att_wave(s - 2)
        if s >= 1:
            z_start(s - 1)
        weigh(s, highest)
        y_start(s)
    weight_copy.wait()
    for w in range(max(slices - 2, 0), end):
        finish(w)
    z_start(end)
    for w in range(max(slices - 2, 0), end):
        gather_start(att_buf, w, a_row + w)
    for w in range(end, slices + nz - 1):
        att_wave(w)
        if 0 <= w - nz < end:
            project_both(w - nz)
    gather_finish(att_buf, end, a_row + end)
    sent = project(end, (1 - core) * half)
    half_send[...] = sent if end == 0 else half_send[...] + sent
    half_copy = pltpu.make_async_remote_copy(
        src_ref=half_send,
        dst_ref=half_recv,
        send_sem=h_send_sem,
        recv_sem=h_recv_sem,
        device_id=(parts_at, me, 1 - core),
        device_id_type=MESH,
    )
    half_copy.start()
    kept = project(end, core * half)
    if end > 0:
        kept = kept + half_keep[...]

    gather_drain(info_buf, 0, 0)
    for s in range(slices):
        gather_drain(q_buf, s, q_row + s)
        gather_drain(att_buf, s, a_row + s)
        for d in range(1, nz + 1):
            y_copy(s, (z + d) % nz).wait_send()
        for d in range(1, nz):
            z_copy(s, (z + d) % nz, z).wait_send()
    half_copy.wait()
    out_ref[...] = (kept + half_recv[...]).astype(BF16)


def local(
    queries,
    block_key_cache,
    block_value_cache,
    new_keys,
    leaf_value_rows,
    ancestors,
    block_slot,
    last_len,
    o_weight,
):
    n = lax.axis_size("blk")
    leaves, features = queries.shape
    ancestry = ancestors.shape[1]
    blocks, block_len, kv_width = block_key_cache.shape
    block_count = blocks * n
    cap = 2 * leaves * ancestry // block_count * n
    slices = SLICES
    nz = n // ROW_PAIR
    heads = kv_width // HEAD_SIZE // slices * PER_GROUP
    width = heads * HEAD_SIZE
    packed = width + HEAD_SIZE
    columns = o_weight.shape[1]

    vmem = pl.BlockSpec(memory_space=pltpu.VMEM)
    anywhere = pl.BlockSpec(memory_space=pl.ANY)
    dma = pltpu.SemaphoreType.DMA
    grows = 1 + 2 * slices
    return pl.pallas_call(
        functools.partial(kernel, n, slices, cap),
        out_shape=jax.ShapeDtypeStruct((n * leaves // 2, columns), BF16),
        in_specs=[vmem] * 6 + [anywhere] * 3,
        out_specs=vmem,
        scratch_shapes=[
            pltpu.VMEM((1, n, 16, HEAD_SIZE), jnp.int32),
            pltpu.VMEM((slices, n, leaves, width), BF16),
            pltpu.VMEM((blocks, block_len, kv_width), BF16),
            pltpu.VMEM((blocks, block_len, kv_width), BF16),
            pltpu.VMEM(o_weight.shape, BF16),
            pltpu.VMEM((blocks, cap, n * leaves), BF16),
            pltpu.VMEM((n * leaves, blocks * cap), BF16),
            pltpu.VMEM((blocks, n * leaves, HEAD_SIZE), BF16),
            pltpu.VMEM((blocks, cap, HEAD_SIZE), F32),
            pltpu.VMEM((blocks, cap, width + 2 * HEAD_SIZE), BF16),
            pltpu.VMEM((blocks, cap, HEAD_SIZE), F32),
            pltpu.VMEM((blocks, cap, HEAD_SIZE), F32),
            pltpu.VMEM((slices, n, leaves, packed), BF16),
            pltpu.VMEM((slices, nz, leaves, packed), BF16),
            pltpu.VMEM((slices, nz, leaves, packed), BF16),
            pltpu.VMEM((slices, nz, leaves, packed), BF16),
            pltpu.VMEM((slices, n, leaves, width), BF16),
            pltpu.VMEM((n * leaves // 2, columns), F32),
            pltpu.VMEM((n * leaves // 2, columns), F32),
            pltpu.VMEM((n * leaves // 2, columns), F32),
            dma((2, blocks)),
            dma,
            dma((grows, n)),
            dma((grows, nz)),
            dma((grows, nz)),
            dma((grows, nz)),
            dma((slices, nz)),
            dma((slices, nz)),
            dma((slices, nz)),
            dma((slices, nz)),
            dma,
            dma,
        ],
        compiler_params=pltpu.CompilerParams(
            collective_id=0, has_side_effects=True, vmem_limit_bytes=56 * 1024 * 1024
        ),
        cost_estimate=pl.CostEstimate(
            flops=4_000_000_000, bytes_accessed=12_000_000, transcendentals=5_000_000
        ),
    )(
        queries,
        ancestors.T,
        last_len[None, :],
        block_slot[None, :],
        new_keys,
        leaf_value_rows,
        block_key_cache,
        block_value_cache,
        o_weight,
    )


def solution(mesh):
    return jax.shard_map(
        local,
        mesh=mesh,
        in_specs=(
            P(("parts", "blk"), "kvh"),
            P(("parts", "blk"), None, "kvh"),
            P(("parts", "blk"), None, "kvh"),
            P(("parts", "blk"), "kvh"),
            P(("parts", "blk"), "kvh"),
            P(("parts", "blk"), None),
            P("parts"),
            P(("parts", "blk")),
            P("kvh", "blk"),
        ),
        out_specs=P(("parts", "kvh"), "blk"),
        check_vma=False,
    )
```
